256 devices in a mesh: ctx: 32 (over y, x, z_lo), ch: 8 (over z_hi, core).
Axes of the slice: x: 4, y: 4, z: 8 (z_hi: 4, z_lo: 2; z = z_hi * 2 + z_lo), core: 2. Of those that a mesh axis runs over, the one named last changes fastest.
Arguments:
- tokens: bfloat16 [65536, 1024], P('ctx', 'ch'), may hold values from -6 to 6
- w_in: bfloat16 [1024, 1024], P(None, 'ch'), may hold values from -0.1875 to 0.1875
- filters: float32 [65536, 24], P('ctx'), may hold values from -0.0234375 to 0.0234375
- w_filter: float32 [24, 1024], P(None, 'ch'), may hold values from -1.25 to 1.25
- w_out: bfloat16 [1024, 1024], P('ch'), may hold values from -0.1875 to 0.1875
Outputs:
- output: bfloat16 [65536, 1024], P('ctx', 'ch')
The draws below stay inside these ranges and needn't reach their ends.
All inputs are finite; a program needn't handle non-finite values.
Results may differ from the reference program's by a relative error of at most 0.0049.
Values may be sent and summed in bfloat16 or wider, within the bound.
No kernel may reach another device: no remote copies, remote signals or barrier semaphores. Data moves between devices by JAX's collectives and lax.ppermute only.
A program may use at most 64 MiB of HBM per device.

```python
import jax
import jax.numpy as jnp
from jax import lax

D = 1024
K = 24
SEQ = 65536
N_CH = 8


def block_levels(own_key, shape, split, least, largest):
    level, own = 1.0, jax.random.fold_in(own_key, 6)
    for dim, blocks in split:
        steps = jnp.exp(jax.random.uniform(jax.random.fold_in(own, dim), (blocks,), jnp.float32, least / len(split), largest / len(split)))
        level = level * jnp.repeat(steps, shape[dim] // blocks).reshape([-1 if axis == dim else 1 for axis in range(len(shape))])
    return level


def noise(rng, extent, spread, limit, split=(), held_as=jnp.bfloat16):
    entries = jax.random.normal(rng, extent, jnp.float32) * spread
    if len(split) > 0:
        entries = block_levels(rng, extent, split, -0.22, 0.18) * entries
    return jnp.clip(entries, min=-limit, max=limit).astype(held_as)


def setup_inputs(seed: int = 0) -> dict:
    key_list = jax.random.split(jax.random.key(seed), 6)
    return {
        "tokens": noise(key_list[0], (SEQ, D), 1.0, 6.0, ((0, 32), (1, 8))),
        "w_in": noise(key_list[1], (D, D), D ** -0.5, 0.1875, ((1, 8),)),
        "filters": noise(key_list[2], (SEQ, K), SEQ ** -0.5, 0.0234375, ((0, 32),), jnp.float32),
        "w_filter": noise(key_list[3], (K, D), K ** -0.5, 1.25, ((1, 8),), jnp.float32),
        "w_out": noise(key_list[4], (D, D), D ** -0.5, 0.1875, ((0, 8),)),
    }


def reference(tokens, w_in, filters, w_filter, w_out):
    projected = jnp.dot(tokens, w_in, preferred_element_type=jnp.float32)
    shaped = jnp.dot(filters, w_filter, precision=lax.Precision.HIGHEST)
    blocks = N_CH
    block_width = D // blocks
    signal_blocks = projected.reshape(SEQ, blocks, block_width).transpose(1, 0, 2)
    kernel_blocks = shaped.reshape(SEQ, blocks, block_width).transpose(1, 0, 2)

    def convolve(both_parts):
        signal_part, kernel_part = both_parts
        spectrum = jnp.fft.rfft(signal_part, n=2 * SEQ, axis=0) * jnp.fft.rfft(kernel_part, n=2 * SEQ, axis=0)
        return jnp.fft.irfft(spectrum, n=2 * SEQ, axis=0)[:SEQ].astype(signal_part.dtype)

    conv = lax.map(convolve, (signal_blocks, kernel_blocks))
    conv = conv.transpose(1, 0, 2).reshape(SEQ, D)
    mixed = conv.astype(jnp.bfloat16)
    return jnp.dot(mixed, w_out, preferred_element_type=jnp.float32).astype(jnp.bfloat16)
```

```python
import math

import jax
import jax.numpy as jnp
import ml_dtypes
import numpy as np
from jax import lax
from jax.experimental import pallas as pl
from jax.experimental.pallas import tpu as pltpu
from jax.sharding import PartitionSpec as P


BF = jnp.bfloat16
F32 = jnp.float32
NB = 256
LANES = 128
VMEM_LIMIT = 56 * 1024 * 1024


def split_np(table):
    table = table.astype(np.float32)
    high = table.astype(ml_dtypes.bfloat16)
    low = (table - high.astype(np.float32)).astype(ml_dtypes.bfloat16)
    return high, low


def tables(ctx_count, ch_count):
    k = np.arange(NB, dtype=np.int64)
    arrive = (np.arange(ctx_count)[None, :] * ch_count + np.arange(ch_count)[:, None]).reshape(-1)
    angle = 2.0 * math.pi / (4 * NB) * (((1 + 4 * k)[:, None] * k[None, :]) % (4 * NB))
    outer = np.concatenate([np.cos(angle), np.sin(angle)], axis=0)
    outer_x = outer[:, arrive]
    back = outer_x.T / (NB * NB)
    angle = 2.0 * math.pi / (4 * NB * NB) * (((1 + 4 * k)[:, None] * k[None, :]) % (4 * NB * NB))
    turn = np.stack([np.cos(angle), np.sin(angle)]).astype(np.float32)
    angle = 2.0 * math.pi / NB * ((k[:, None] * k[None, :]) % NB)
    cos, sin = np.cos(angle), np.sin(angle)
    inner = np.block([[cos, sin], [-sin, cos]])
    inner_back = np.block([[cos, -sin], [sin, cos]])
    return (
        np.stack(split_np(outer)),
        np.stack(split_np(outer_x)),
        np.stack(split_np(inner)),
        np.stack(split_np(inner_back)),
        np.stack(split_np(back)),
        turn,
    )


def dot(a, b, dims=((1,), (0,))):
    return lax.dot_general(a, b, (dims, ((), ())), preferred_element_type=F32)


def split(x):
    high = x.astype(BF)
    return high, (x - high.astype(F32)).astype(BF)


def shape_kernel(filters_ref, w_ref, out_ref, wide_ref):
    fh, fl = split(filters_ref[...])
    wh, wl = split(w_ref[...])
    dims = ((0,), (1,))
    shaped = dot(wh, fh, dims) + (dot(wl, fh, dims) + dot(wh, fl, dims))
    rows = wide_ref.shape[0] // 32
    for block in range(shaped.shape[1] // LANES):
        m, half = divmod(block, 2)
        for c in range(4):
            wide_ref[pl.ds(m * 8 + c * 2 + half, 32, stride=rows), :] = shaped[
                32 * c : 32 * (c + 1), block * LANES : (block + 1) * LANES
            ]
    out_ref[...] = wide_ref[...].astype(out_ref.dtype)


def project_kernel(tokens_ref, w_ref, out_ref, wide_ref):
    count = tokens_ref.shape[0] // NB
    tokens = jnp.concatenate([tokens_ref[pl.ds(NB * j, NB), :] for j in range(count)], axis=1)
    for j in range(count):
        part = dot(w_ref[pl.ds(LANES * j, LANES), :], tokens, ((1,), (1,)))
        for c in range(4):
            for half in range(2):
                wide_ref[pl.ds(j * 256 + c * 2 + half, 32, stride=8), :] = part[
                    32 * c : 32 * (c + 1), half * LANES : (half + 1) * LANES
                ]
    out_ref[...] = wide_ref[...].astype(out_ref.dtype)


def forward(wide_ref, outer_ref, inner_ref, turn_ref, c):
    x = jnp.concatenate(
        [wide_ref[pl.ds(c * 2 + half, NB, stride=8), :] for half in range(2)], axis=1
    ).astype(BF)
    first = dot(outer_ref[0], x) + dot(outer_ref[1], x)
    re, im = first[:NB], first[NB:]
    cos, sin = turn_ref[0], turn_ref[1]
    turned = jnp.concatenate([re * cos - im * sin, re * sin + im * cos], axis=1)
    high, low = split(turned)
    return dot(high, inner_ref[0]) + (dot(low, inner_ref[0]) + dot(high, inner_ref[1]))


def filter_kernel(h_ref, outer_ref, inner_ref, turn_ref, out_ref, wide_ref):
    wide_ref[...] = h_ref[...].astype(F32)
    for c in range(4):
        out_ref[c] = forward(wide_ref, outer_ref, inner_ref, turn_ref, c)


def conv_kernel(
    x_ref, spec_ref, outer_ref, inner_ref, inner_back_ref, back_ref, turn_ref, out_ref, wide_ref
):
    wide_ref[...] = x_ref[...].astype(F32)
    cos, sin = turn_ref[0], turn_ref[1]
    for c in range(4):
        got = forward(wide_ref, outer_ref, inner_ref, turn_ref, c)
        re, im = got[:, :NB], got[:, NB:]
        hre, him = spec_ref[c, :, :NB], spec_ref[c, :, NB:]
        high, low = split(jnp.concatenate([re * hre - im * him, re * him + im * hre], axis=1))
        half = dot(high, inner_back_ref[0]) + (
            dot(low, inner_back_ref[0]) + dot(high, inner_back_ref[1])
        )
        re, im = half[:, :NB], half[:, NB:]
        high, low = split(jnp.concatenate([re * cos + im * sin, im * cos - re * sin], axis=0))
        y = dot(back_ref[0], high) + (dot(back_ref[0], low) + dot(back_ref[1], high))
        for part in range(2):
            wide_ref[pl.ds(c * 2 + part, NB, stride=8), :] = y[
                :, part * LANES : (part + 1) * LANES
            ]
    out_ref[...] = wide_ref[...].astype(out_ref.dtype)


def output_kernel(mixed_ref, w_ref, out_ref, wide_ref):
    wide_ref[...] = mixed_ref[...].astype(F32)
    count = out_ref.shape[0] // NB
    rows = []
    for j in range(count):
        for c in range(4):
            rows.append(
                jnp.concatenate(
                    [
                        wide_ref[pl.ds(j * 256 + c * 2 + half, 32, stride=8), :]
                        for half in range(2)
                    ],
                    axis=1,
                )
            )
    mixed = jnp.concatenate(rows, axis=0).astype(BF)
    result = dot(mixed, w_ref[...], ((0,), (0,))).astype(out_ref.dtype)
    for j in range(count):
        out_ref[pl.ds(NB * j, NB), :] = result[:, j * LANES : (j + 1) * LANES]


def call(kernel, shape, dtype, wide, flops, *args):
    size = sum(a.size * a.dtype.itemsize for a in args) + math.prod(shape) * 4
    return pl.pallas_call(
        kernel,
        out_shape=jax.ShapeDtypeStruct(shape, dtype),
        scratch_shapes=[pltpu.VMEM(wide, F32)],
        compiler_params=pltpu.CompilerParams(vmem_limit_bytes=VMEM_LIMIT),
        cost_estimate=pl.CostEstimate(flops=flops, bytes_accessed=size, transcendentals=0),
    )(*args)


def local(tokens, w_in, filters, w_filter, w_out):
    ctx_count, ch_count = lax.axis_size("ctx"), lax.axis_size("ch")
    every = ("ch", "ctx")
    outer, outer_x, inner, inner_back, back, turn = tables(ctx_count, ch_count)
    wide = tokens.shape
    w_in = lax.all_gather(w_in.T, "ch", axis=0, tiled=True)
    w_out = lax.all_gather(w_out, "ch", axis=0, tiled=True)
    tokens = lax.all_to_all(tokens, "ch", 0, 0, tiled=True)
    shaped = call(shape_kernel, wide, BF, wide, 2**25, filters, w_filter)
    shaped = lax.all_to_all(shaped, "ctx", 0, 0, tiled=True)
    spectrum = call(
        filter_kernel, (4, NB, 2 * NB), F32, wide, 2**31, shaped, outer, inner, turn
    )
    signal = call(project_kernel, wide, BF, wide, 2**29, tokens, w_in)
    signal = lax.all_to_all(signal, every, 0, 0, tiled=True)
    mixed = call(
        conv_kernel, wide, BF, wide, 2**32, signal, spectrum, outer_x, inner, inner_back, back, turn
    )
    mixed = lax.all_to_all(mixed, every, 0, 0, tiled=True)
    result = call(output_kernel, wide, BF, wide, 2**29, mixed, w_out)
    return lax.all_to_all(result, "ch", 0, 0, tiled=True)


def solution(mesh):
    placed = (P("ctx", "ch"), P(None, "ch"), P("ctx", None), P(None, "ch"), P("ch", None))
    return jax.shard_map(
        local, mesh=mesh, in_specs=placed, out_specs=P("ctx", "ch"), check_vma=False
    )
```

```python
import math

import jax
import jax.numpy as jnp
import ml_dtypes
import numpy as np
from jax import lax
from jax.experimental import pallas as pl
from jax.experimental.pallas import tpu as pltpu
from jax.sharding import PartitionSpec as P


BF = jnp.bfloat16
F32 = jnp.float32
NB = 256
LANES = 128
VMEM_LIMIT = 24 * 1024 * 1024


def split_np(table):
    table = table.astype(np.float32)
    high = table.astype(ml_dtypes.bfloat16)
    low = (table - high.astype(np.float32)).astype(ml_dtypes.bfloat16)
    return high, low


def tables(ctx_count, ch_count):
    k = np.arange(NB, dtype=np.int64)
    arrive = (np.arange(ctx_count)[None, :] * ch_count + np.arange(ch_count)[:, None]).reshape(-1)
    angle = 2.0 * math.pi / (4 * NB) * (((1 + 4 * k)[:, None] * k[None, :]) % (4 * NB))
    outer = np.concatenate([np.cos(angle), np.sin(angle)], axis=0)
    outer_x = outer[:, arrive]
    back = (outer_x * np.repeat([1.0, -1.0], NB)[:, None]).T / (NB * NB)
    angle = 2.0 * math.pi / (4 * NB * NB) * (((1 + 4 * k)[:, None] * k[None, :]) % (4 * NB * NB))
    turn = np.stack([np.cos(angle), np.sin(angle)]).astype(np.float32)
    angle = 2.0 * math.pi / NB * ((k[:, None] * k[None, :]) % NB)
    cos, sin = np.cos(angle), np.sin(angle)
    inner = np.block([[cos, sin], [-sin, cos]])
    return (
        np.stack(split_np(outer)),
        np.stack(split_np(outer_x)),
        np.stack(split_np(inner)),
        np.stack(split_np(back)),
        turn,
    )


def dot(a, b, dims=((1,), (0,))):
    return lax.dot_general(a, b, (dims, ((), ())), preferred_element_type=F32)


def split(x):
    high = x.astype(BF)
    return high, (x - high.astype(F32)).astype(BF)


def weight_rows(place_ref, part_ref, z):
    z_back = (place_ref[1] - z + 4) % 4
    return jnp.concatenate(
        [
            part_ref[pl.ds(pl.multiple_of(((place_ref[2] - q + 4) % 4 * 4 + z_back) * 32, 32), 32), :]
            for q in range(4)
        ],
        axis=0,
    )


def shape_kernel(filters_ref, w_ref, out_ref, wide_ref):
    fh, fl = split(filters_ref[...])
    wh, wl = split(w_ref[...])
    dims = ((0,), (1,))
    shaped = dot(wh, fh, dims) + (dot(wl, fh, dims) + dot(wh, fl, dims))
    rows = wide_ref.shape[0] // 32
    for block in range(shaped.shape[1] // LANES):
        m, half = divmod(block, 2)
        for c in range(4):
            wide_ref[pl.ds(m * 8 + c * 2 + half, 32, stride=rows), :] = shaped[
                32 * c : 32 * (c + 1), block * LANES : (block + 1) * LANES
            ]
    out_ref[...] = wide_ref[...].astype(out_ref.dtype)


def project_kernel(place_ref, tokens_ref, own_ref, mate_ref, out_ref, wide_ref):
    count = tokens_ref.shape[0] // NB
    tokens = jnp.concatenate([tokens_ref[pl.ds(NB * j, NB), :] for j in range(count)], axis=1)
    for rel, part_ref in enumerate((own_ref, mate_ref)):
        for z in range(count // 2):
            j = 2 * z + (place_ref[0] + rel) % 2
            part = dot(weight_rows(place_ref, part_ref, z), tokens, ((1,), (1,)))
            for c in range(4):
                for half in range(2):
                    wide_ref[j, pl.ds(c * 2 + half, 32, stride=8), :] = part[
                        32 * c : 32 * (c + 1), half * LANES : (half + 1) * LANES
                    ]
    for j in range(count):
        out_ref[pl.ds(NB * j, NB), :] = wide_ref[j].astype(out_ref.dtype)


def spread(re, im, turn_ref, axis):
    cos, sin = turn_ref[0], turn_ref[1]
    return split(jnp.concatenate([re * cos - im * sin, re * sin + im * cos], axis=axis))


def inner_product(high, low, inner_ref):
    return dot(high, inner_ref[0]) + (dot(low, inner_ref[0]) + dot(high, inner_ref[1]))


def first_product(wide_ref, outer_ref, c):
    x = jnp.concatenate(
        [wide_ref[pl.ds(c * 2 + half, NB, stride=8), :] for half in range(2)], axis=1
    ).astype(BF)
    return dot(outer_ref[0], x) + dot(outer_ref[1], x)


def filter_kernel(h_ref, outer_ref, inner_ref, turn_ref, out_ref, wide_ref):
    wide_ref[...] = h_ref[...].astype(F32)
    for c in range(4):
        first = first_product(wide_ref, outer_ref, c)
        out_ref[c] = inner_product(*spread(first[:NB], first[NB:], turn_ref, 1), inner_ref)


def conv_kernel(*refs):
    sources, out_ref, wide_ref, held, sem = refs[:6], refs[6], refs[7], refs[8:14], refs[14]
    pairs = list(zip(sources, held))[:5] + [(sources[5].at[c], held[5].at[c]) for c in range(4)]
    copies = [pltpu.make_async_copy(*pair, sem.at[n]) for n, pair in enumerate(pairs)]
    for n in (0, 1, 2, 3, 5, 4):
        copies[n].start()
    x_ref, outer_ref, turn_ref, inner_ref, back_ref, spec_ref = held
    copies[0].wait()
    wide_ref[...] = x_ref[...].astype(F32)
    copies[1].wait()
    for n in (6, 7, 8):
        copies[n].start()
    for c in range(4):
        first = first_product(wide_ref, outer_ref, c)
        if c == 0:
            copies[2].wait()
        high, low = spread(first[:NB], first[NB:], turn_ref, 1)
        if c == 0:
            copies[3].wait()
        got = inner_product(high, low, inner_ref)
        copies[5 + c].wait()
        re, im = got[:, :NB], got[:, NB:]
        hre, him = spec_ref[c, :, :NB], spec_ref[c, :, NB:]
        high, low = split(jnp.concatenate([re * hre - im * him, -(re * him + im * hre)], axis=1))
        half = inner_product(high, low, inner_ref)
        high, low = spread(half[:, :NB], half[:, NB:], turn_ref, 0)
        if c == 0:
            copies[4].wait()
        y = dot(back_ref[0], high) + (dot(back_ref[0], low) + dot(back_ref[1], high))
        for part in range(2):
            wide_ref[pl.ds(c * 2 + part, NB, stride=8), :] = y[
                :, part * LANES : (part + 1) * LANES
            ]
    out_ref[...] = wide_ref[...].astype(out_ref.dtype)


def output_kernel(place_ref, mixed_ref, own_ref, mate_ref, out_ref, wide_ref):
    count = out_ref.shape[0] // NB
    for j in range(count):
        wide_ref[j] = mixed_ref[pl.ds(NB * j, NB), :].astype(F32)
    rows, weights = [], []
    for rel, part_ref in enumerate((own_ref, mate_ref)):
        for z in range(count // 2):
            j = 2 * z + (place_ref[0] + rel) % 2
            weights.append(weight_rows(place_ref, part_ref, z))
            for c in range(4):
                rows.append(
                    jnp.concatenate(
                        [wide_ref[j, pl.ds(c * 2 + half, 32, stride=8), :] for half in range(2)],
                        axis=1,
                    )
                )
    mixed = jnp.concatenate(rows, axis=0).astype(BF)
    result = dot(mixed, jnp.concatenate(weights, axis=0), ((0,), (0,))).astype(out_ref.dtype)
    for j in range(count):
        out_ref[pl.ds(NB * j, NB), :] = result[:, j * LANES : (j + 1) * LANES]


def call(kernel, shape, dtype, wide, flops, *args, scalars=False, fetched=None, limit=VMEM_LIMIT):
    size = sum(a.size * a.dtype.itemsize for a in args) + math.prod(shape) * 4
    space = pltpu.VMEM if fetched is None else pl.ANY
    specs = [pl.BlockSpec(memory_space=space)] * len(args)
    if scalars:
        specs[0] = pl.BlockSpec(memory_space=pltpu.SMEM)
    scratch = [pltpu.VMEM(wide, F32)]
    if fetched is not None:
        scratch = scratch + fetched
    return pl.pallas_call(
        kernel,
        out_shape=jax.ShapeDtypeStruct(shape, dtype),
        in_specs=specs,
        out_specs=pl.BlockSpec(memory_space=pltpu.VMEM),
        scratch_shapes=scratch,
        compiler_params=pltpu.CompilerParams(
            vmem_limit_bytes=limit
        ),
        cost_estimate=pl.CostEstimate(flops=flops, bytes_accessed=size, transcendentals=0),
    )(*args)


def over_z(x, step):
    return lax.ppermute(x, "ch", [(n, (n + 2 * step) % 8) for n in range(8)])


def over_core(x):
    return lax.ppermute(x, "ch", [(n, n ^ 1) for n in range(8)])


def over_plane(x, step_y, step_x):
    pairs = []
    for n in range(32):
        y, rest = divmod(n, 8)
        x_place, z_low = divmod(rest, 2)
        pairs.append((n, (y + step_y) % 4 * 8 + (x_place + step_x) % 4 * 2 + z_low))
    return lax.ppermute(x, "ctx", pairs)


def gather_rows(rows):
    rows = jnp.concatenate([rows, over_z(rows, 1), over_z(rows, 2), over_z(rows, -1)])
    rows = jnp.concatenate(
        [rows, over_plane(rows, 0, 1), over_plane(rows, 1, 0), over_plane(rows, 0, -1)]
    )
    return rows, over_core(rows)


def local(tokens, w_in, filters, w_filter, w_out):
    ctx_count, ch_count = lax.axis_size("ctx"), lax.axis_size("ch")
    ctx_place, ch_place = lax.axis_index("ctx"), lax.axis_index("ch")
    every = ("ch", "ctx")
    outer, outer_x, inner, back, turn = tables(ctx_count, ch_count)
    wide = tokens.shape
    blocks = (ch_count, wide[0] // ch_count, wide[1])
    quarter = (ctx_place // 2 % 4 + 2 * (ctx_place // 8)) % 4
    place = jnp.stack([ch_place % 2, ch_place // 2, quarter]).astype(jnp.int32)
    in_own, in_mate = gather_rows(lax.dynamic_slice_in_dim(w_in, 32 * quarter, 32, 1).T)
    tokens = lax.all_to_all(tokens, "ch", 0, 0, tiled=True)
    shaped = call(shape_kernel, wide, BF, wide, 2**25, filters, w_filter)
    shaped = lax.all_to_all(shaped, "ctx", 0, 0, tiled=True)
    spectrum = call(
        filter_kernel, (4, NB, 2 * NB), F32, wide, 2**31, shaped, outer, inner, turn
    )
    w_out, tokens = lax.optimization_barrier((w_out, tokens))
    out_own, out_mate = gather_rows(lax.dynamic_slice_in_dim(w_out, 32 * quarter, 32, 0))
    signal = call(
        project_kernel, wide, BF, blocks, 2**29, place, tokens, in_own, in_mate, scalars=True
    )
    signal = lax.all_to_all(signal, every, 0, 0, tiled=True)
    operands = [signal, outer_x, turn, inner, back, spectrum]
    fetched = [pltpu.VMEM(a.shape, a.dtype) for a in operands] + [pltpu.SemaphoreType.DMA((9,))]
    mixed = call(
        conv_kernel, wide, BF, wide, 2**32, *operands, fetched=fetched, limit=60 * 2**20
    )
    mixed = lax.all_to_all(mixed, every, 0, 0, tiled=True)
    result = call(
        output_kernel, wide, BF, blocks, 2**29, place, mixed, out_own, out_mate, scalars=True
    )
    return lax.all_to_all(result, "ch", 0, 0, tiled=True)


def solution(mesh):
    placed = (P("ctx", "ch"), P(None, "ch"), P("ctx", None), P(None, "ch"), P("ch", None))
    return jax.shard_map(
        local, mesh=mesh, in_specs=placed, out_specs=P("ctx", "ch"), check_vma=False
    )
```

```python
import math

import jax
import jax.numpy as jnp
import ml_dtypes
import numpy as np
from jax import lax
from jax.experimental import pallas as pl
from jax.experimental.pallas import tpu as pltpu
from jax.sharding import PartitionSpec as P


BF = jnp.bfloat16
F32 = jnp.float32
NB = 256
LANES = 128
VMEM_LIMIT = 24 * 1024 * 1024


def split_np(table):
    table = table.astype(np.float32)
    high = table.astype(ml_dtypes.bfloat16)
    low = (table - high.astype(np.float32)).astype(ml_dtypes.bfloat16)
    return high, low


def tables(ctx_count, ch_count):
    k = np.arange(NB, dtype=np.int64)
    arrive = (np.arange(ctx_count)[None, :] * ch_count + np.arange(ch_count)[:, None]).reshape(-1)
    angle = 2.0 * math.pi / (4 * NB) * (((1 + 4 * k)[:, None] * k[None, :]) % (4 * NB))
    outer = np.concatenate([np.cos(angle), np.sin(angle)], axis=0)
    outer_x = outer[:, arrive]
    back = (outer_x * np.repeat([1.0, -1.0], NB)[:, None]).T / (NB * NB)
    angle = 2.0 * math.pi / (4 * NB * NB) * (((1 + 4 * k)[:, None] * k[None, :]) % (4 * NB * NB))
    turn = np.stack([np.cos(angle), np.sin(angle)]).astype(np.float32)
    angle = 2.0 * math.pi / NB * ((k[:, None] * k[None, :]) % NB)
    cos, sin = np.cos(angle), np.sin(angle)
    inner = np.block([[cos, sin], [-sin, cos]])
    return (
        np.stack(split_np(outer)),
        np.stack(split_np(outer_x)),
        np.stack(split_np(inner)),
        np.stack(split_np(back)),
        turn,
    )


def dot(a, b, dims=((1,), (0,))):
    return lax.dot_general(a, b, (dims, ((), ())), preferred_element_type=F32)


def split(x):
    high = x.astype(BF)
    return high, (x - high.astype(F32)).astype(BF)


def weight_rows(place_ref, part_ref, z):
    z_back = (place_ref[1] - z + 4) % 4
    return jnp.concatenate(
        [
            part_ref[pl.ds(pl.multiple_of(((place_ref[2] - q + 4) % 4 * 4 + z_back) * 32, 32), 32), :]
            for q in range(4)
        ],
        axis=0,
    )


def shape_kernel(filters_ref, w_ref, out_ref, wide_ref):
    fh, fl = split(filters_ref[...])
    wh, wl = split(w_ref[...])
    dims = ((0,), (1,))
    shaped = dot(wh, fh, dims) + (dot(wl, fh, dims) + dot(wh, fl, dims))
    rows = wide_ref.shape[0] // 32
    for block in range(shaped.shape[1] // LANES):
        m, half = divmod(block, 2)
        for c in range(4):
            wide_ref[pl.ds(m * 8 + c * 2 + half, 32, stride=rows), :] = shaped[
                32 * c : 32 * (c + 1), block * LANES : (block + 1) * LANES
            ]
    out_ref[...] = wide_ref[...].astype(out_ref.dtype)


def project_kernel(place_ref, tokens_ref, own_ref, mate_ref, out_ref, wide_ref):
    count = tokens_ref.shape[0] // NB
    tokens = jnp.concatenate([tokens_ref[pl.ds(NB * j, NB), :] for j in range(count)], axis=1)
    for rel, part_ref in enumerate((own_ref, mate_ref)):
        for z in range(count // 2):
            j = 2 * z + (place_ref[0] + rel) % 2
            part = dot(weight_rows(place_ref, part_ref, z), tokens, ((1,), (1,)))
            for c in range(4):
                for half in range(2):
                    wide_ref[j, pl.ds(c * 2 + half, 32, stride=8), :] = part[
                        32 * c : 32 * (c + 1), half * LANES : (half + 1) * LANES
                    ]
    for j in range(count):
        out_ref[pl.ds(NB * j, NB), :] = wide_ref[j].astype(out_ref.dtype)


def spread(re, im, turn_ref, axis):
    cos, sin = turn_ref[0], turn_ref[1]
    return split(jnp.concatenate([re * cos - im * sin, re * sin + im * cos], axis=axis))


def inner_product(high, low, inner_ref):
    return dot(high, inner_ref[0]) + (dot(low, inner_ref[0]) + dot(high, inner_ref[1]))


def first_product(wide_ref, outer_ref, c):
    x = jnp.concatenate(
        [wide_ref[pl.ds(c * 2 + half, NB, stride=8), :] for half in range(2)], axis=1
    ).astype(BF)
    return dot(outer_ref[0], x) + dot(outer_ref[1], x)


def filter_kernel(h_ref, outer_ref, inner_ref, turn_ref, out_ref, wide_ref):
    wide_ref[...] = h_ref[...].astype(F32)
    for c in range(4):
        first = first_product(wide_ref, outer_ref, c)
        out_ref[c] = inner_product(*spread(first[:NB], first[NB:], turn_ref, 1), inner_ref)


def conv_kernel(*refs):
    sources, out_ref, wide_ref, held, sem = refs[:6], refs[6], refs[7], refs[8:14], refs[14]
    pairs = list(zip(sources, held))[:5] + [(sources[5].at[c], held[5].at[c]) for c in range(4)]
    copies = [pltpu.make_async_copy(*pair, sem.at[n]) for n, pair in enumerate(pairs)]
    for n in (0, 1, 2, 3, 5, 4):
        copies[n].start()
    x_ref, outer_ref, turn_ref, inner_ref, back_ref, spec_ref = held
    copies[0].wait()
    wide_ref[...] = x_ref[...].astype(F32)
    copies[1].wait()
    for n in (6, 7, 8):
        copies[n].start()
    for c in range(4):
        first = first_product(wide_ref, outer_ref, c)
        if c == 0:
            copies[2].wait()
        high, low = spread(first[:NB], first[NB:], turn_ref, 1)
        if c == 0:
            copies[3].wait()
        got = inner_product(high, low, inner_ref)
        copies[5 + c].wait()
        re, im = got[:, :NB], got[:, NB:]
        hre, him = spec_ref[c, :, :NB], spec_ref[c, :, NB:]
        high, low = split(jnp.concatenate([re * hre - im * him, -(re * him + im * hre)], axis=1))
        half = inner_product(high, low, inner_ref)
        high, low = spread(half[:, :NB], half[:, NB:], turn_ref, 0)
        if c == 0:
            copies[4].wait()
        y = dot(back_ref[0], high) + (dot(back_ref[0], low) + dot(back_ref[1], high))
        for part in range(2):
            wide_ref[pl.ds(c * 2 + part, NB, stride=8), :] = y[
                :, part * LANES : (part + 1) * LANES
            ]
    out_ref[...] = wide_ref[...].astype(out_ref.dtype)


def output_kernel(place_ref, mixed_ref, own_ref, mate_ref, out_ref, wide_ref):
    count = out_ref.shape[0] // NB
    for j in range(count):
        wide_ref[j] = mixed_ref[pl.ds(NB * j, NB), :].astype(F32)
    rows, weights = [], []
    for rel, part_ref in enumerate((own_ref, mate_ref)):
        for z in range(count // 2):
            j = 2 * z + (place_ref[0] + rel) % 2
            weights.append(weight_rows(place_ref, part_ref, z))
            for c in range(4):
                rows.append(
                    jnp.concatenate(
                        [wide_ref[j, pl.ds(c * 2 + half, 32, stride=8), :] for half in range(2)],
                        axis=1,
                    )
                )
    mixed = jnp.concatenate(rows, axis=0).astype(BF)
    result = dot(mixed, jnp.concatenate(weights, axis=0), ((0,), (0,))).astype(out_ref.dtype)
    for j in range(count):
        out_ref[pl.ds(NB * j, NB), :] = result[:, j * LANES : (j + 1) * LANES]


def call(kernel, shape, dtype, wide, flops, *args, scalars=False, fetched=None, limit=VMEM_LIMIT):
    size = sum(a.size * a.dtype.itemsize for a in args) + math.prod(shape) * 4
    space = pltpu.VMEM if fetched is None else pl.ANY
    specs = [pl.BlockSpec(memory_space=space)] * len(args)
    if scalars:
        specs[0] = pl.BlockSpec(memory_space=pltpu.SMEM)
    scratch = [pltpu.VMEM(wide, F32)]
    if fetched is not None:
        scratch = scratch + fetched
    return pl.pallas_call(
        kernel,
        out_shape=jax.ShapeDtypeStruct(shape, dtype),
        in_specs=specs,
        out_specs=pl.BlockSpec(memory_space=pltpu.VMEM),
        scratch_shapes=scratch,
        compiler_params=pltpu.CompilerParams(
            vmem_limit_bytes=limit
        ),
        cost_estimate=pl.CostEstimate(flops=flops, bytes_accessed=size, transcendentals=0),
    )(*args)


def over_z(x, step):
    return lax.ppermute(x, "ch", [(n, (n + 2 * step) % 8) for n in range(8)])


def over_core(x):
    return lax.ppermute(x, "ch", [(n, n ^ 1) for n in range(8)])


def over_plane(x, step_y, step_x):
    pairs = []
    for n in range(32):
        y, rest = divmod(n, 8)
        x_place, z_low = divmod(rest, 2)
        pairs.append((n, (y + step_y) % 4 * 8 + (x_place + step_x) % 4 * 2 + z_low))
    return lax.ppermute(x, "ctx", pairs)


def gather_plane(rows):
    rows = jnp.concatenate(
        [rows, over_plane(rows, 0, 1), over_plane(rows, 1, 0), over_plane(rows, 0, -1)]
    )
    return rows


def local(tokens, w_in, filters, w_filter, w_out):
    ctx_count, ch_count = lax.axis_size("ctx"), lax.axis_size("ch")
    ctx_place, ch_place = lax.axis_index("ctx"), lax.axis_index("ch")
    every = ("ch", "ctx")
    outer, outer_x, inner, back, turn = tables(ctx_count, ch_count)
    wide = tokens.shape
    blocks = (ch_count, wide[0] // ch_count, wide[1])
    quarter = (ctx_place // 2 % 4 + 2 * (ctx_place // 8)) % 4
    place = jnp.stack([ch_place % 2, ch_place // 2, quarter]).astype(jnp.int32)
    shaped = call(shape_kernel, wide, BF, wide, 2**25, filters, w_filter)
    w_in, w_out, shaped = lax.optimization_barrier((w_in, w_out, shaped))
    rows = jnp.concatenate(
        [
            lax.dynamic_slice_in_dim(w_in, 32 * quarter, 32, 1).T,
            lax.dynamic_slice_in_dim(w_out, 32 * quarter, 32, 0),
        ]
    )
    shaped = lax.all_to_all(shaped, "ctx", 0, 0, tiled=True)
    rows = jnp.stack([rows, over_z(rows, 1), over_z(rows, 2), over_z(rows, -1)])
    tokens, shaped, rows = lax.optimization_barrier((tokens, shaped, rows))
    in_rows = rows[:, :32].reshape(128, -1)
    out_rows = rows[:, 32:].reshape(128, -1)
    tokens = lax.all_to_all(tokens, "ch", 0, 0, tiled=True)
    in_own = gather_plane(in_rows)
    tokens, in_own = lax.optimization_barrier((tokens, in_own))
    in_mate = over_core(in_own)
    signal = call(
        project_kernel, wide, BF, blocks, 2**29, place, tokens, in_own, in_mate, scalars=True
    )
    out_rows, signal, shaped = lax.optimization_barrier((out_rows, signal, shaped))
    spectrum = call(
        filter_kernel, (4, NB, 2 * NB), F32, wide, 2**31, shaped, outer, inner, turn
    )
    out_own = gather_plane(out_rows)
    out_mate = over_core(out_own)
    signal = lax.all_to_all(signal, every, 0, 0, tiled=True)
    operands = [signal, outer_x, turn, inner, back, spectrum]
    fetched = [pltpu.VMEM(a.shape, a.dtype) for a in operands] + [pltpu.SemaphoreType.DMA((9,))]
    mixed = call(
        conv_kernel, wide, BF, wide, 2**32, *operands, fetched=fetched, limit=60 * 2**20
    )
    mixed = lax.all_to_all(mixed, every, 0, 0, tiled=True)
    result = call(
        output_kernel, wide, BF, blocks, 2**29, place, mixed, out_own, out_mate, scalars=True
    )
    return lax.all_to_all(result, "ch", 0, 0, tiled=True)


def solution(mesh):
    placed = (P("ctx", "ch"), P(None, "ch"), P("ctx", None), P(None, "ch"), P("ch", None))
    return jax.shard_map(
        local, mesh=mesh, in_specs=placed, out_specs=P("ctx", "ch"), check_vma=False
    )
```

```python
import math

import jax
import jax.numpy as jnp
import ml_dtypes
import numpy as np
from jax import lax
from jax.experimental import pallas as pl
from jax.experimental.pallas import tpu as pltpu
from jax.sharding import PartitionSpec as P


BF = jnp.bfloat16
F32 = jnp.float32
NB = 256
LANES = 128
VMEM_LIMIT = 24 * 1024 * 1024


def split_np(table):
    table = table.astype(np.float32)
    high = table.astype(ml_dtypes.bfloat16)
    low = (table - high.astype(np.float32)).astype(ml_dtypes.bfloat16)
    return high, low


def tables(ctx_count, ch_count):
    k = np.arange(NB, dtype=np.int64)
    arrive = (np.arange(ctx_count)[None, :] * ch_count + np.arange(ch_count)[:, None]).reshape(-1)
    angle = 2.0 * math.pi / (4 * NB) * (((1 + 4 * k)[:, None] * k[None, :]) % (4 * NB))
    outer = np.concatenate([np.cos(angle), np.sin(angle)], axis=0)
    outer_x = outer[:, arrive]
    back = (outer_x * np.repeat([1.0, -1.0], NB)[:, None]).T / (NB * NB)
    angle = 2.0 * math.pi / (4 * NB * NB) * (((1 + 4 * k)[:, None] * k[None, :]) % (4 * NB * NB))
    turn = np.stack([np.cos(angle), np.sin(angle)]).astype(np.float32)
    angle = 2.0 * math.pi / NB * ((k[:, None] * k[None, :]) % NB)
    cos, sin = np.cos(angle), np.sin(angle)
    inner = np.block([[cos, sin], [-sin, cos]])
    return (
        np.stack(split_np(outer)),
        np.stack(split_np(outer_x)),
        np.stack(split_np(inner)),
        np.stack(split_np(back)),
        turn,
    )


def dot(a, b, dims=((1,), (0,))):
    return lax.dot_general(a, b, (dims, ((), ())), preferred_element_type=F32)


def split(x):
    high = x.astype(BF)
    return high, (x - high.astype(F32)).astype(BF)


def weight_rows(place_ref, part_ref, z):
    z_back = (place_ref[1] - z + 4) % 4
    return jnp.concatenate(
        [
            part_ref[pl.ds(pl.multiple_of(((place_ref[2] - q + 4) % 4 * 4 + z_back) * 32, 32), 32), :]
            for q in range(4)
        ],
        axis=0,
    )


def shape_kernel(filters_ref, w_ref, out_ref, wide_ref):
    fh, fl = split(filters_ref[...])
    wh, wl = split(w_ref[...])
    dims = ((0,), (1,))
    shaped = dot(wh, fh, dims) + (dot(wl, fh, dims) + dot(wh, fl, dims))
    rows = wide_ref.shape[0] // 32
    for block in range(shaped.shape[1] // LANES):
        m, half = divmod(block, 2)
        for c in range(4):
            wide_ref[pl.ds(m * 8 + c * 2 + half, 32, stride=rows), :] = shaped[
                32 * c : 32 * (c + 1), block * LANES : (block + 1) * LANES
            ]
    out_ref[...] = wide_ref[...].astype(out_ref.dtype)


def project_kernel(place_ref, tokens_ref, own_ref, mate_ref, out_ref, wide_ref):
    count = tokens_ref.shape[0] // NB
    tokens = jnp.concatenate([tokens_ref[pl.ds(NB * j, NB), :] for j in range(count)], axis=1)
    for rel, part_ref in enumerate((own_ref, mate_ref)):
        for z in range(count // 2):
            j = 2 * z + (place_ref[0] + rel) % 2
            part = dot(weight_rows(place_ref, part_ref, z), tokens, ((1,), (1,)))
            for c in range(4):
                for half in range(2):
                    wide_ref[j, pl.ds(c * 2 + half, 32, stride=8), :] = part[
                        32 * c : 32 * (c + 1), half * LANES : (half + 1) * LANES
                    ]
    for j in range(count):
        out_ref[pl.ds(NB * j, NB), :] = wide_ref[j].astype(out_ref.dtype)


def spread(re, im, turn_ref, axis):
    cos, sin = turn_ref[0], turn_ref[1]
    return split(jnp.concatenate([re * cos - im * sin, re * sin + im * cos], axis=axis))


def inner_product(high, low, inner_ref):
    return dot(high, inner_ref[0]) + (dot(low, inner_ref[0]) + dot(high, inner_ref[1]))


def first_product(wide_ref, outer_ref):
    x = jnp.concatenate([wide_ref[pl.ds(n, NB, stride=8), :] for n in range(8)], axis=1)
    x = x.astype(BF)
    return dot(outer_ref[0], x) + dot(outer_ref[1], x)


def channel(values, c):
    return values[:, c * NB : (c + 1) * NB]


def rows_of_channels(first, turn_ref):
    pairs = [
        spread(channel(first[:NB], c), channel(first[NB:], c), turn_ref, 1) for c in range(4)
    ]
    return [jnp.concatenate(part, axis=0) for part in zip(*pairs)]


def filter_kernel(h_ref, outer_ref, inner_ref, turn_ref, out_ref, wide_ref):
    wide_ref[...] = h_ref[...].astype(F32)
    high, low = rows_of_channels(first_product(wide_ref, outer_ref), turn_ref)
    out_ref[...] = inner_product(high, low, inner_ref)


def conv_kernel(*refs):
    sources, out_ref, wide_ref, held, sem = refs[:6], refs[6], refs[7], refs[8:14], refs[14]
    copies = [
        pltpu.make_async_copy(source, into, sem.at[n])
        for n, (source, into) in enumerate(zip(sources, held))
    ]
    for copy in copies:
        copy.start()
    x_ref, outer_ref, turn_ref, inner_ref, spec_ref, back_ref = held
    copies[0].wait()
    wide_ref[...] = x_ref[...].astype(F32)
    copies[1].wait()
    first = first_product(wide_ref, outer_ref)
    copies[2].wait()
    high, low = rows_of_channels(first, turn_ref)
    copies[3].wait()
    got = inner_product(high, low, inner_ref)
    copies[4].wait()
    re, im = got[:, :NB], got[:, NB:]
    hre, him = spec_ref[:, :NB], spec_ref[:, NB:]
    high, low = split(jnp.concatenate([re * hre - im * him, -(re * him + im * hre)], axis=1))
    half = inner_product(high, low, inner_ref)
    pairs = [
        spread(half[c * NB : (c + 1) * NB, :NB], half[c * NB : (c + 1) * NB, NB:], turn_ref, 0)
        for c in range(4)
    ]
    high, low = [jnp.concatenate(part, axis=1) for part in zip(*pairs)]
    copies[5].wait()
    y = dot(back_ref[0], high) + (dot(back_ref[0], low) + dot(back_ref[1], high))
    for n in range(8):
        wide_ref[pl.ds(n, NB, stride=8), :] = y[:, n * LANES : (n + 1) * LANES]
    out_ref[...] = wide_ref[...].astype(out_ref.dtype)


def output_kernel(place_ref, mixed_ref, own_ref, mate_ref, out_ref, wide_ref):
    count = out_ref.shape[0] // NB
    for j in range(count):
        wide_ref[j] = mixed_ref[pl.ds(NB * j, NB), :].astype(F32)
    rows, weights = [], []
    for rel, part_ref in enumerate((own_ref, mate_ref)):
        for z in range(count // 2):
            j = 2 * z + (place_ref[0] + rel) % 2
            weights.append(weight_rows(place_ref, part_ref, z))
            for c in range(4):
                rows.append(
                    jnp.concatenate(
                        [wide_ref[j, pl.ds(c * 2 + half, 32, stride=8), :] for half in range(2)],
                        axis=1,
                    )
                )
    mixed = jnp.concatenate(rows, axis=0).astype(BF)
    result = dot(mixed, jnp.concatenate(weights, axis=0), ((0,), (0,))).astype(out_ref.dtype)
    for j in range(count):
        out_ref[pl.ds(NB * j, NB), :] = result[:, j * LANES : (j + 1) * LANES]


def call(kernel, shape, dtype, wide, flops, *args, scalars=False, fetched=None, limit=VMEM_LIMIT):
    size = sum(a.size * a.dtype.itemsize for a in args) + math.prod(shape) * 4
    space = pltpu.VMEM if fetched is None else pl.ANY
    specs = [pl.BlockSpec(memory_space=space)] * len(args)
    if scalars:
        specs[0] = pl.BlockSpec(memory_space=pltpu.SMEM)
    scratch = [pltpu.VMEM(wide, F32)]
    if fetched is not None:
        scratch = scratch + fetched
    return pl.pallas_call(
        kernel,
        out_shape=jax.ShapeDtypeStruct(shape, dtype),
        in_specs=specs,
        out_specs=pl.BlockSpec(memory_space=pltpu.VMEM),
        scratch_shapes=scratch,
        compiler_params=pltpu.CompilerParams(
            vmem_limit_bytes=limit
        ),
        cost_estimate=pl.CostEstimate(flops=flops, bytes_accessed=size, transcendentals=0),
    )(*args)


def over_z(x, step):
    return lax.ppermute(x, "ch", [(n, (n + 2 * step) % 8) for n in range(8)])


def over_core(x):
    return lax.ppermute(x, "ch", [(n, n ^ 1) for n in range(8)])


def over_plane(x, step_y, step_x):
    pairs = []
    for n in range(32):
        y, rest = divmod(n, 8)
        x_place, z_low = divmod(rest, 2)
        pairs.append((n, (y + step_y) % 4 * 8 + (x_place + step_x) % 4 * 2 + z_low))
    return lax.ppermute(x, "ctx", pairs)


def gather_rows(rows):
    rows = jnp.concatenate([rows, over_z(rows, 1), over_z(rows, 2), over_z(rows, -1)])
    rows = jnp.concatenate(
        [rows, over_plane(rows, 0, 1), over_plane(rows, 1, 0), over_plane(rows, 0, -1)]
    )
    return rows, over_core(rows)


def local(tokens, w_in, filters, w_filter, w_out):
    ctx_count, ch_count = lax.axis_size("ctx"), lax.axis_size("ch")
    ctx_place, ch_place = lax.axis_index("ctx"), lax.axis_index("ch")
    every = ("ch", "ctx")
    outer, outer_x, inner, back, turn = tables(ctx_count, ch_count)
    wide = tokens.shape
    blocks = (ch_count, wide[0] // ch_count, wide[1])
    quarter = (ctx_place // 2 % 4 + 2 * (ctx_place // 8)) % 4
    place = jnp.stack([ch_place % 2, ch_place // 2, quarter]).astype(jnp.int32)
    in_own, in_mate = gather_rows(lax.dynamic_slice_in_dim(w_in, 32 * quarter, 32, 1).T)
    tokens = lax.all_to_all(tokens, "ch", 0, 0, tiled=True)
    shaped = call(shape_kernel, wide, BF, wide, 2**25, filters, w_filter)
    shaped = lax.all_to_all(shaped, "ctx", 0, 0, tiled=True)
    spectrum = call(
        filter_kernel, (4 * NB, 2 * NB), F32, wide, 2**31, shaped, outer, inner, turn
    )
    w_out, tokens = lax.optimization_barrier((w_out, tokens))
    out_own, out_mate = gather_rows(lax.dynamic_slice_in_dim(w_out, 32 * quarter, 32, 0))
    signal = call(
        project_kernel, wide, BF, blocks, 2**29, place, tokens, in_own, in_mate, scalars=True
    )
    signal = lax.all_to_all(signal, every, 0, 0, tiled=True)
    operands = [signal, outer_x, turn, inner, spectrum, back]
    fetched = [pltpu.VMEM(a.shape, a.dtype) for a in operands] + [pltpu.SemaphoreType.DMA((6,))]
    mixed = call(
        conv_kernel, wide, BF, wide, 2**32, *operands, fetched=fetched, limit=60 * 2**20
    )
    mixed = lax.all_to_all(mixed, every, 0, 0, tiled=True)
    result = call(
        output_kernel, wide, BF, blocks, 2**29, place, mixed, out_own, out_mate, scalars=True
    )
    return lax.all_to_all(result, "ch", 0, 0, tiled=True)


def solution(mesh):
    placed = (P("ctx", "ch"), P(None, "ch"), P("ctx", None), P(None, "ch"), P("ch", None))
    return jax.shard_map(
        local, mesh=mesh, in_specs=placed, out_specs=P("ctx", "ch"), check_vma=False
    )
```

```python
import math

import jax
import jax.numpy as jnp
import ml_dtypes
import numpy as np
from jax import lax
from jax.experimental import pallas as pl
from jax.experimental.pallas import tpu as pltpu
from jax.sharding import PartitionSpec as P


BF = jnp.bfloat16
F32 = jnp.float32
NB = 256
LANES = 128
VMEM_LIMIT = 24 * 1024 * 1024


def split_np(table):
    table = table.astype(np.float32)
    high = table.astype(ml_dtypes.bfloat16)
    low = (table - high.astype(np.float32)).astype(ml_dtypes.bfloat16)
    return high, low


def tables(ctx_count, ch_count):
    k = np.arange(NB, dtype=np.int64)
    arrive = (np.arange(ctx_count)[None, :] * ch_count + np.arange(ch_count)[:, None]).reshape(-1)
    angle = 2.0 * math.pi / (4 * NB) * (((1 + 4 * k)[:, None] * k[None, :]) % (4 * NB))
    outer = np.concatenate([np.cos(angle), np.sin(angle)], axis=0)
    outer_x = outer[:, arrive]
    back = (outer_x * np.repeat([1.0, -1.0], NB)[:, None]).T / (NB * NB)
    angle = 2.0 * math.pi / (4 * NB * NB) * (((1 + 4 * k)[:, None] * k[None, :]) % (4 * NB * NB))
    turn = np.stack([np.cos(angle), np.sin(angle)]).astype(np.float32)
    angle = 2.0 * math.pi / NB * ((k[:, None] * k[None, :]) % NB)
    cos, sin = np.cos(angle), np.sin(angle)
    inner = np.block([[cos, sin], [-sin, cos]])
    return (
        np.stack(split_np(outer)),
        np.stack(split_np(outer_x)),
        np.stack(split_np(inner)),
        np.stack(split_np(back)),
        turn,
    )


def dot(a, b, dims=((1,), (0,))):
    return lax.dot_general(a, b, (dims, ((), ())), preferred_element_type=F32)


def split(x):
    high = x.astype(BF)
    return high, (x - high.astype(F32)).astype(BF)


def weight_rows(place_ref, part_ref, z):
    z_back = (place_ref[1] - z + 4) % 4
    return jnp.concatenate(
        [
            part_ref[pl.ds(pl.multiple_of(((place_ref[2] - q + 4) % 4 * 4 + z_back) * 32, 32), 32), :]
            for q in range(4)
        ],
        axis=0,
    )


def shape_kernel(filters_ref, w_ref, out_ref, wide_ref):
    fh, fl = split(filters_ref[...])
    wh, wl = split(w_ref[...])
    dims = ((0,), (1,))
    shaped = dot(wh, fh, dims) + (dot(wl, fh, dims) + dot(wh, fl, dims))
    rows = wide_ref.shape[0] // 32
    for block in range(shaped.shape[1] // LANES):
        m, half = divmod(block, 2)
        for c in range(4):
            wide_ref[pl.ds(m * 8 + c * 2 + half, 32, stride=rows), :] = shaped[
                32 * c : 32 * (c + 1), block * LANES : (block + 1) * LANES
            ]
    out_ref[...] = wide_ref[...].astype(out_ref.dtype)


def project_kernel(place_ref, tokens_ref, own_ref, mate_ref, out_ref, wide_ref):
    count = tokens_ref.shape[0] // NB
    tokens = jnp.concatenate([tokens_ref[pl.ds(NB * j, NB), :] for j in range(count)], axis=1)
    for rel, part_ref in enumerate((own_ref, mate_ref)):
        for z in range(count // 2):
            j = 2 * z + (place_ref[0] + rel) % 2
            part = dot(weight_rows(place_ref, part_ref, z), tokens, ((1,), (1,)))
            for c in range(4):
                for half in range(2):
                    wide_ref[j, pl.ds(c * 2 + half, 32, stride=8), :] = part[
                        32 * c : 32 * (c + 1), half * LANES : (half + 1) * LANES
                    ]
    for j in range(count):
        out_ref[pl.ds(NB * j, NB), :] = wide_ref[j].astype(out_ref.dtype)


def spread(re, im, turn_ref, axis):
    cos, sin = turn_ref[0], turn_ref[1]
    return split(jnp.concatenate([re * cos - im * sin, re * sin + im * cos], axis=axis))


def inner_product(high, low, inner_ref):
    return dot(high, inner_ref[0]) + (dot(low, inner_ref[0]) + dot(high, inner_ref[1]))


def first_product(wide_ref, outer_ref):
    x = jnp.concatenate([wide_ref[pl.ds(n, NB, stride=8), :] for n in range(8)], axis=1)
    x = x.astype(BF)
    return dot(outer_ref[0], x) + dot(outer_ref[1], x)


def channel(values, c):
    return values[:, c * NB : (c + 1) * NB]


def rows_of_channels(first, turn_ref):
    pairs = [
        spread(channel(first[:NB], c), channel(first[NB:], c), turn_ref, 1) for c in range(4)
    ]
    return [jnp.concatenate(part, axis=0) for part in zip(*pairs)]


def filter_kernel(h_ref, outer_ref, inner_ref, turn_ref, out_ref, wide_ref):
    wide_ref[...] = h_ref[...].astype(F32)
    high, low = rows_of_channels(first_product(wide_ref, outer_ref), turn_ref)
    out_ref[...] = inner_product(high, low, inner_ref)


def conv_kernel(*refs):
    sources, out_ref, wide_ref, held, sem = refs[:6], refs[6], refs[7], refs[8:14], refs[14]
    copies = [
        pltpu.make_async_copy(source, into, sem.at[n])
        for n, (source, into) in enumerate(zip(sources, held))
    ]
    for copy in copies:
        copy.start()
    x_ref, outer_ref, turn_ref, inner_ref, spec_ref, back_ref = held
    copies[0].wait()
    wide_ref[...] = x_ref[...].astype(F32)
    copies[1].wait()
    first = first_product(wide_ref, outer_ref)
    copies[2].wait()
    high, low = rows_of_channels(first, turn_ref)
    copies[3].wait()
    got = inner_product(high, low, inner_ref)
    copies[4].wait()
    re, im = got[:, :NB], got[:, NB:]
    hre, him = spec_ref[:, :NB], spec_ref[:, NB:]
    high, low = split(jnp.concatenate([re * hre - im * him, -(re * him + im * hre)], axis=1))
    half = inner_product(high, low, inner_ref)
    pairs = [
        spread(half[c * NB : (c + 1) * NB, :NB], half[c * NB : (c + 1) * NB, NB:], turn_ref, 0)
        for c in range(4)
    ]
    high, low = [jnp.concatenate(part, axis=1) for part in zip(*pairs)]
    copies[5].wait()
    y = dot(back_ref[0], high) + (dot(back_ref[0], low) + dot(back_ref[1], high))
    for n in range(8):
        wide_ref[pl.ds(n, NB, stride=8), :] = y[:, n * LANES : (n + 1) * LANES]
    out_ref[...] = wide_ref[...].astype(out_ref.dtype)


def output_kernel(place_ref, mixed_ref, own_ref, mate_ref, out_ref, wide_ref):
    count = out_ref.shape[0] // NB
    for j in range(count):
        wide_ref[j] = mixed_ref[pl.ds(NB * j, NB), :].astype(F32)
    rows, weights = [], []
    for rel, part_ref in enumerate((own_ref, mate_ref)):
        for z in range(count // 2):
            j = 2 * z + (place_ref[0] + rel) % 2
            weights.append(weight_rows(place_ref, part_ref, z))
            for c in range(4):
                rows.append(
                    jnp.concatenate(
                        [wide_ref[j, pl.ds(c * 2 + half, 32, stride=8), :] for half in range(2)],
                        axis=1,
                    )
                )
    mixed = jnp.concatenate(rows, axis=0).astype(BF)
    result = dot(mixed, jnp.concatenate(weights, axis=0), ((0,), (0,))).astype(out_ref.dtype)
    for j in range(count):
        out_ref[pl.ds(NB * j, NB), :] = result[:, j * LANES : (j + 1) * LANES]


def call(kernel, shape, dtype, wide, flops, *args, scalars=False, fetched=None, limit=VMEM_LIMIT):
    size = sum(a.size * a.dtype.itemsize for a in args) + math.prod(shape) * 4
    space = pltpu.VMEM if fetched is None else pl.ANY
    specs = [pl.BlockSpec(memory_space=space)] * len(args)
    if scalars:
        specs[0] = pl.BlockSpec(memory_space=pltpu.SMEM)
    scratch = [pltpu.VMEM(wide, F32)]
    if fetched is not None:
        scratch = scratch + fetched
    return pl.pallas_call(
        kernel,
        out_shape=jax.ShapeDtypeStruct(shape, dtype),
        in_specs=specs,
        out_specs=pl.BlockSpec(memory_space=pltpu.VMEM),
        scratch_shapes=scratch,
        compiler_params=pltpu.CompilerParams(
            vmem_limit_bytes=limit
        ),
        cost_estimate=pl.CostEstimate(flops=flops, bytes_accessed=size, transcendentals=0),
    )(*args)


def over_z(x, step):
    return lax.ppermute(x, "ch", [(n, (n + 2 * step) % 8) for n in range(8)])


def over_core(x):
    return lax.ppermute(x, "ch", [(n, n ^ 1) for n in range(8)])


def over_plane(x, step_y, step_x):
    pairs = []
    for n in range(32):
        y, rest = divmod(n, 8)
        x_place, z_low = divmod(rest, 2)
        pairs.append((n, (y + step_y) % 4 * 8 + (x_place + step_x) % 4 * 2 + z_low))
    return lax.ppermute(x, "ctx", pairs)


def gather_rows(rows, relay):
    below, above = over_z(rows, 1), over_z(rows, -1)
    across = over_z(below, 1) if relay else over_z(rows, 2)
    rows = jnp.concatenate([rows, below, across, above])
    rows = jnp.concatenate(
        [rows, over_plane(rows, 0, 1), over_plane(rows, 1, 0), over_plane(rows, 0, -1)]
    )
    return rows, over_core(rows)


def local(tokens, w_in, filters, w_filter, w_out):
    ctx_count, ch_count = lax.axis_size("ctx"), lax.axis_size("ch")
    ctx_place, ch_place = lax.axis_index("ctx"), lax.axis_index("ch")
    every = ("ch", "ctx")
    outer, outer_x, inner, back, turn = tables(ctx_count, ch_count)
    wide = tokens.shape
    blocks = (ch_count, wide[0] // ch_count, wide[1])
    quarter = (ctx_place // 2 % 4 + 2 * (ctx_place // 8)) % 4
    place = jnp.stack([ch_place % 2, ch_place // 2, quarter]).astype(jnp.int32)
    in_own, in_mate = gather_rows(lax.dynamic_slice_in_dim(w_in, 32 * quarter, 32, 1).T, True)
    tokens = lax.all_to_all(tokens, "ch", 0, 0, tiled=True)
    shaped = call(shape_kernel, wide, BF, wide, 2**25, filters, w_filter)
    shaped = lax.all_to_all(shaped, "ctx", 0, 0, tiled=True)
    spectrum = call(
        filter_kernel, (4 * NB, 2 * NB), F32, wide, 2**31, shaped, outer, inner, turn
    )
    w_out, tokens = lax.optimization_barrier((w_out, tokens))
    out_own, out_mate = gather_rows(lax.dynamic_slice_in_dim(w_out, 32 * quarter, 32, 0), False)
    signal = call(
        project_kernel, wide, BF, blocks, 2**29, place, tokens, in_own, in_mate, scalars=True
    )
    signal = lax.all_to_all(signal, every, 0, 0, tiled=True)
    operands = [signal, outer_x, turn, inner, spectrum, back]
    fetched = [pltpu.VMEM(a.shape, a.dtype) for a in operands] + [pltpu.SemaphoreType.DMA((6,))]
    mixed = call(
        conv_kernel, wide, BF, wide, 2**32, *operands, fetched=fetched, limit=60 * 2**20
    )
    mixed = lax.all_to_all(mixed, every, 0, 0, tiled=True)
    result = call(
        output_kernel, wide, BF, blocks, 2**29, place, mixed, out_own, out_mate, scalars=True
    )
    return lax.all_to_all(result, "ch", 0, 0, tiled=True)


def solution(mesh):
    placed = (P("ctx", "ch"), P(None, "ch"), P("ctx", None), P(None, "ch"), P("ch", None))
    return jax.shard_map(
        local, mesh=mesh, in_specs=placed, out_specs=P("ctx", "ch"), check_vma=False
    )
```

```python
import math

import jax
import jax.numpy as jnp
import ml_dtypes
import numpy as np
from jax import lax
from jax.experimental import pallas as pl
from jax.experimental.pallas import tpu as pltpu
from jax.sharding import PartitionSpec as P


BF = jnp.bfloat16
F32 = jnp.float32
NB = 256
LANES = 128
VMEM_LIMIT = 24 * 1024 * 1024


def split_np(table):
    table = table.astype(np.float32)
    high = table.astype(ml_dtypes.bfloat16)
    low = (table - high.astype(np.float32)).astype(ml_dtypes.bfloat16)
    return high, low


def tables(ctx_count, ch_count):
    k = np.arange(NB, dtype=np.int64)
    arrive = (np.arange(ctx_count)[None, :] * ch_count + np.arange(ch_count)[:, None]).reshape(-1)
    angle = 2.0 * math.pi / (4 * NB) * (((1 + 4 * k)[:, None] * k[None, :]) % (4 * NB))
    outer = np.concatenate([np.cos(angle), np.sin(angle)], axis=0)
    outer_x = outer[:, arrive]
    back = (outer_x * np.repeat([1.0, -1.0], NB)[:, None]).T / (NB * NB)
    angle = 2.0 * math.pi / (4 * NB * NB) * (((1 + 4 * k)[:, None] * k[None, :]) % (4 * NB * NB))
    turn = np.stack([np.cos(angle), np.sin(angle)]).astype(np.float32)
    angle = 2.0 * math.pi / NB * ((k[:, None] * k[None, :]) % NB)
    cos, sin = np.cos(angle), np.sin(angle)
    inner = np.block([[cos, sin], [-sin, cos]])
    return (
        np.stack(split_np(outer)),
        np.stack(split_np(outer_x)),
        np.stack(split_np(inner)),
        np.stack(split_np(back)),
        turn,
    )


def dot(a, b, dims=((1,), (0,))):
    return lax.dot_general(a, b, (dims, ((), ())), preferred_element_type=F32)


def split(x):
    high = x.astype(BF)
    return high, (x - high.astype(F32)).astype(BF)


def weight_rows(place_ref, part_ref, z):
    z_back = (place_ref[1] - z + 4) % 4
    return jnp.concatenate(
        [
            part_ref[pl.ds(pl.multiple_of(((place_ref[2] - q + 4) % 4 * 4 + z_back) * 32, 32), 32), :]
            for q in range(4)
        ],
        axis=0,
    )


def shape_kernel(filters_ref, w_ref, out_ref, wide_ref):
    fh, fl = split(filters_ref[...])
    wh, wl = split(w_ref[...])
    dims = ((0,), (1,))
    shaped = dot(wh, fh, dims) + (dot(wl, fh, dims) + dot(wh, fl, dims))
    rows = wide_ref.shape[0] // 32
    for block in range(shaped.shape[1] // LANES):
        m, half = divmod(block, 2)
        for c in range(4):
            wide_ref[pl.ds(m * 8 + c * 2 + half, 32, stride=rows), :] = shaped[
                32 * c : 32 * (c + 1), block * LANES : (block + 1) * LANES
            ]
    out_ref[...] = wide_ref[...].astype(out_ref.dtype)


def project_kernel(place_ref, tokens_ref, own_ref, mate_ref, out_ref, wide_ref):
    count = tokens_ref.shape[0] // NB
    tokens = jnp.concatenate([tokens_ref[pl.ds(NB * j, NB), :] for j in range(count)], axis=1)
    places = [(rel, z) for rel in range(2) for z in range(count // 2)]
    parts = (own_ref, mate_ref)
    weight = jnp.concatenate([weight_rows(place_ref, parts[rel], z) for rel, z in places], axis=0)
    result = dot(weight, tokens, ((1,), (1,)))
    for n, (rel, z) in enumerate(places):
        j = 2 * z + (place_ref[0] + rel) % 2
        for c in range(4):
            row = n * LANES + 32 * c
            for half in range(2):
                wide_ref[j, pl.ds(c * 2 + half, 32, stride=8), :] = result[
                    row : row + 32, half * LANES : (half + 1) * LANES
                ]
    for j in range(count):
        out_ref[pl.ds(NB * j, NB), :] = wide_ref[j].astype(out_ref.dtype)


def spread(re, im, turn_ref, axis):
    cos, sin = turn_ref[0], turn_ref[1]
    return split(jnp.concatenate([re * cos - im * sin, re * sin + im * cos], axis=axis))


def inner_product(high, low, inner_ref):
    return dot(high, inner_ref[0]) + (dot(low, inner_ref[0]) + dot(high, inner_ref[1]))


def first_product(wide_ref, outer_ref):
    x = jnp.concatenate([wide_ref[pl.ds(n, NB, stride=8), :] for n in range(8)], axis=1)
    x = x.astype(BF)
    return dot(outer_ref[0], x) + dot(outer_ref[1], x)


def channel(values, c):
    return values[:, c * NB : (c + 1) * NB]


def rows_of_channels(first, turn_ref):
    pairs = [
        spread(channel(first[:NB], c), channel(first[NB:], c), turn_ref, 1) for c in range(4)
    ]
    return [jnp.concatenate(part, axis=0) for part in zip(*pairs)]


def filter_kernel(h_ref, outer_ref, inner_ref, turn_ref, out_ref, wide_ref):
    wide_ref[...] = h_ref[...].astype(F32)
    high, low = rows_of_channels(first_product(wide_ref, outer_ref), turn_ref)
    out_ref[...] = inner_product(high, low, inner_ref)


def conv_kernel(*refs):
    sources, out_ref, wide_ref, held, sem = refs[:6], refs[6], refs[7], refs[8:14], refs[14]
    copies = [
        pltpu.make_async_copy(source, into, sem.at[n])
        for n, (source, into) in enumerate(zip(sources, held))
    ]
    for copy in copies:
        copy.start()
    x_ref, outer_ref, turn_ref, inner_ref, spec_ref, back_ref = held
    copies[0].wait()
    wide_ref[...] = x_ref[...].astype(F32)
    copies[1].wait()
    first = first_product(wide_ref, outer_ref)
    copies[2].wait()
    high, low = rows_of_channels(first, turn_ref)
    copies[3].wait()
    got = inner_product(high, low, inner_ref)
    copies[4].wait()
    re, im = got[:, :NB], got[:, NB:]
    hre, him = spec_ref[:, :NB], spec_ref[:, NB:]
    high, low = split(jnp.concatenate([re * hre - im * him, -(re * him + im * hre)], axis=1))
    half = inner_product(high, low, inner_ref)
    pairs = [
        spread(half[c * NB : (c + 1) * NB, :NB], half[c * NB : (c + 1) * NB, NB:], turn_ref, 0)
        for c in range(4)
    ]
    high, low = [jnp.concatenate(part, axis=1) for part in zip(*pairs)]
    copies[5].wait()
    y = dot(back_ref[0], high) + (dot(back_ref[0], low) + dot(back_ref[1], high))
    for n in range(8):
        wide_ref[pl.ds(n, NB, stride=8), :] = y[:, n * LANES : (n + 1) * LANES]
    out_ref[...] = wide_ref[...].astype(out_ref.dtype)


def output_kernel(place_ref, mixed_ref, own_ref, mate_ref, out_ref, wide_ref):
    count = out_ref.shape[0] // NB
    for j in range(count):
        wide_ref[j] = mixed_ref[pl.ds(NB * j, NB), :].astype(F32)
    rows, weights = [], []
    for rel, part_ref in enumerate((own_ref, mate_ref)):
        for z in range(count // 2):
            j = 2 * z + (place_ref[0] + rel) % 2
            weights.append(weight_rows(place_ref, part_ref, z))
            for c in range(4):
                rows.append(
                    jnp.concatenate(
                        [wide_ref[j, pl.ds(c * 2 + half, 32, stride=8), :] for half in range(2)],
                        axis=1,
                    )
                )
    mixed = jnp.concatenate(rows, axis=0).astype(BF)
    result = dot(mixed, jnp.concatenate(weights, axis=0), ((0,), (0,))).astype(out_ref.dtype)
    for j in range(count):
        out_ref[pl.ds(NB * j, NB), :] = result[:, j * LANES : (j + 1) * LANES]


def call(kernel, shape, dtype, wide, flops, *args, scalars=False, fetched=None, limit=VMEM_LIMIT):
    size = sum(a.size * a.dtype.itemsize for a in args) + math.prod(shape) * 4
    space = pltpu.VMEM if fetched is None else pl.ANY
    specs = [pl.BlockSpec(memory_space=space)] * len(args)
    if scalars:
        specs[0] = pl.BlockSpec(memory_space=pltpu.SMEM)
    scratch = [pltpu.VMEM(wide, F32)]
    if fetched is not None:
        scratch = scratch + fetched
    return pl.pallas_call(
        kernel,
        out_shape=jax.ShapeDtypeStruct(shape, dtype),
        in_specs=specs,
        out_specs=pl.BlockSpec(memory_space=pltpu.VMEM),
        scratch_shapes=scratch,
        compiler_params=pltpu.CompilerParams(
            vmem_limit_bytes=limit
        ),
        cost_estimate=pl.CostEstimate(flops=flops, bytes_accessed=size, transcendentals=0),
    )(*args)


def over_z(x, step):
    return lax.ppermute(x, "ch", [(n, (n + 2 * step) % 8) for n in range(8)])


def over_core(x):
    return lax.ppermute(x, "ch", [(n, n ^ 1) for n in range(8)])


def over_plane(x, step_y, step_x):
    pairs = []
    for n in range(32):
        y, rest = divmod(n, 8)
        x_place, z_low = divmod(rest, 2)
        pairs.append((n, (y + step_y) % 4 * 8 + (x_place + step_x) % 4 * 2 + z_low))
    return lax.ppermute(x, "ctx", pairs)


def gather_rows(rows):
    rows = jnp.concatenate([rows, over_z(rows, 1), over_z(rows, 2), over_z(rows, -1)])
    rows = jnp.concatenate(
        [rows, over_plane(rows, 0, 1), over_plane(rows, 1, 0), over_plane(rows, 0, -1)]
    )
    return rows, over_core(rows)


def local(tokens, w_in, filters, w_filter, w_out):
    ctx_count, ch_count = lax.axis_size("ctx"), lax.axis_size("ch")
    ctx_place, ch_place = lax.axis_index("ctx"), lax.axis_index("ch")
    every = ("ch", "ctx")
    outer, outer_x, inner, back, turn = tables(ctx_count, ch_count)
    wide = tokens.shape
    blocks = (ch_count, wide[0] // ch_count, wide[1])
    quarter = (ctx_place // 2 % 4 + 2 * (ctx_place // 8)) % 4
    place = jnp.stack([ch_place % 2, ch_place // 2, quarter]).astype(jnp.int32)
    in_own, in_mate = gather_rows(lax.dynamic_slice_in_dim(w_in, 32 * quarter, 32, 1).T)
    tokens = lax.all_to_all(tokens, "ch", 0, 0, tiled=True)
    shaped = call(shape_kernel, wide, BF, wide, 2**25, filters, w_filter)
    shaped = lax.all_to_all(shaped, "ctx", 0, 0, tiled=True)
    spectrum = call(
        filter_kernel, (4 * NB, 2 * NB), F32, wide, 2**31, shaped, outer, inner, turn
    )
    w_out, tokens = lax.optimization_barrier((w_out, tokens))
    out_own, out_mate = gather_rows(lax.dynamic_slice_in_dim(w_out, 32 * quarter, 32, 0))
    signal = call(
        project_kernel, wide, BF, blocks, 2**29, place, tokens, in_own, in_mate, scalars=True
    )
    signal = lax.all_to_all(signal, every, 0, 0, tiled=True)
    operands = [signal, outer_x, turn, inner, spectrum, back]
    fetched = [pltpu.VMEM(a.shape, a.dtype) for a in operands] + [pltpu.SemaphoreType.DMA((6,))]
    mixed = call(
        conv_kernel, wide, BF, wide, 2**32, *operands, fetched=fetched, limit=60 * 2**20
    )
    mixed = lax.all_to_all(mixed, every, 0, 0, tiled=True)
    result = call(
        output_kernel, wide, BF, blocks, 2**29, place, mixed, out_own, out_mate, scalars=True
    )
    return lax.all_to_all(result, "ch", 0, 0, tiled=True)


def solution(mesh):
    placed = (P("ctx", "ch"), P(None, "ch"), P("ctx", None), P(None, "ch"), P("ch", None))
    return jax.shard_map(
        local, mesh=mesh, in_specs=placed, out_specs=P("ctx", "ch"), check_vma=False
    )
```

```python
import math

import jax
import jax.numpy as jnp
import ml_dtypes
import numpy as np
from jax import lax
from jax.experimental import pallas as pl
from jax.experimental.pallas import tpu as pltpu
from jax.sharding import PartitionSpec as P


BF = jnp.bfloat16
F32 = jnp.float32
NB = 256
LANES = 128
VMEM_LIMIT = 24 * 1024 * 1024


def split_np(table):
    table = table.astype(np.float32)
    high = table.astype(ml_dtypes.bfloat16)
    low = (table - high.astype(np.float32)).astype(ml_dtypes.bfloat16)
    return high, low


def tables(ctx_count, ch_count):
    k = np.arange(NB, dtype=np.int64)
    arrive = (np.arange(ctx_count)[None, :] * ch_count + np.arange(ch_count)[:, None]).reshape(-1)
    angle = 2.0 * math.pi / (4 * NB) * (((1 + 4 * k)[:, None] * k[None, :]) % (4 * NB))
    outer = np.concatenate([np.cos(angle), np.sin(angle)], axis=0)
    outer_x = outer[:, arrive]
    back = (outer_x * np.repeat([1.0, -1.0], NB)[:, None]).T / (NB * NB)
    angle = 2.0 * math.pi / (4 * NB * NB) * (((1 + 4 * k)[:, None] * k[None, :]) % (4 * NB * NB))
    turn = np.stack([np.cos(angle), np.sin(angle)]).astype(np.float32)
    angle = 2.0 * math.pi / NB * ((k[:, None] * k[None, :]) % NB)
    cos, sin = np.cos(angle), np.sin(angle)
    inner = np.block([[cos, sin], [-sin, cos]])
    return (
        np.stack(split_np(outer)),
        np.stack(split_np(outer_x)),
        np.stack(split_np(inner)),
        np.stack(split_np(back)),
        turn,
    )


def dot(a, b, dims=((1,), (0,))):
    return lax.dot_general(a, b, (dims, ((), ())), preferred_element_type=F32)


def split(x):
    high = x.astype(BF)
    return high, (x - high.astype(F32)).astype(BF)


def weight_rows(place_ref, part_ref, z, group=4, first=0):
    z_back = (place_ref[1] - z + 4) % 4
    return jnp.concatenate(
        [
            part_ref[pl.ds(pl.multiple_of(((place_ref[2] - q + 4) % 4 * group + first + z_back) * 32, 32), 32), :]
            for q in range(4)
        ],
        axis=0,
    )


def shape_kernel(filters_ref, w_ref, out_ref, wide_ref):
    fh, fl = split(filters_ref[...])
    wh, wl = split(w_ref[...])
    dims = ((0,), (1,))
    shaped = dot(wh, fh, dims) + (dot(wl, fh, dims) + dot(wh, fl, dims))
    rows = wide_ref.shape[0] // 32
    for block in range(shaped.shape[1] // LANES):
        m, half = divmod(block, 2)
        for c in range(4):
            wide_ref[pl.ds(m * 8 + c * 2 + half, 32, stride=rows), :] = shaped[
                32 * c : 32 * (c + 1), block * LANES : (block + 1) * LANES
            ]
    out_ref[...] = wide_ref[...].astype(out_ref.dtype)


def project_kernel(place_ref, tokens_ref, own_ref, mate_ref, out_ref, wide_ref):
    count = tokens_ref.shape[0] // NB
    tokens = jnp.concatenate([tokens_ref[pl.ds(NB * j, NB), :] for j in range(count)], axis=1)
    places = [(rel, z) for rel in range(2) for z in range(count // 2)]
    parts = (own_ref, mate_ref)
    weight = jnp.concatenate([weight_rows(place_ref, parts[rel], z) for rel, z in places], axis=0)
    result = dot(weight, tokens, ((1,), (1,)))
    for n, (rel, z) in enumerate(places):
        j = 2 * z + (place_ref[0] + rel) % 2
        for c in range(4):
            row = n * LANES + 32 * c
            for half in range(2):
                wide_ref[j, pl.ds(c * 2 + half, 32, stride=8), :] = result[
                    row : row + 32, half * LANES : (half + 1) * LANES
                ]
    for j in range(count):
        out_ref[pl.ds(NB * j, NB), :] = wide_ref[j].astype(out_ref.dtype)


def spread(re, im, turn_ref, axis):
    cos, sin = turn_ref[0], turn_ref[1]
    return split(jnp.concatenate([re * cos - im * sin, re * sin + im * cos], axis=axis))


def inner_product(high, low, inner_ref):
    return dot(high, inner_ref[0]) + (dot(low, inner_ref[0]) + dot(high, inner_ref[1]))


def first_product(wide_ref, outer_ref):
    x = jnp.concatenate([wide_ref[pl.ds(n, NB, stride=8), :] for n in range(8)], axis=1)
    x = x.astype(BF)
    return dot(outer_ref[0], x) + dot(outer_ref[1], x)


def channel(values, c):
    return values[:, c * NB : (c + 1) * NB]


def rows_of_channels(first, turn_ref):
    pairs = [
        spread(channel(first[:NB], c), channel(first[NB:], c), turn_ref, 1) for c in range(4)
    ]
    return [jnp.concatenate(part, axis=0) for part in zip(*pairs)]


def filter_kernel(h_ref, outer_ref, inner_ref, turn_ref, out_ref, wide_ref):
    wide_ref[...] = h_ref[...].astype(F32)
    high, low = rows_of_channels(first_product(wide_ref, outer_ref), turn_ref)
    out_ref[...] = inner_product(high, low, inner_ref)


def conv_kernel(*refs):
    sources, out_ref, wide_ref, held, sem = refs[:6], refs[6], refs[7], refs[8:14], refs[14]
    copies = [
        pltpu.make_async_copy(source, into, sem.at[n])
        for n, (source, into) in enumerate(zip(sources, held))
    ]
    for copy in copies:
        copy.start()
    x_ref, outer_ref, turn_ref, inner_ref, spec_ref, back_ref = held
    copies[0].wait()
    wide_ref[...] = x_ref[...].astype(F32)
    copies[1].wait()
    first = first_product(wide_ref, outer_ref)
    copies[2].wait()
    high, low = rows_of_channels(first, turn_ref)
    copies[3].wait()
    got = inner_product(high, low, inner_ref)
    copies[4].wait()
    re, im = got[:, :NB], got[:, NB:]
    hre, him = spec_ref[:, :NB], spec_ref[:, NB:]
    high, low = split(jnp.concatenate([re * hre - im * him, -(re * him + im * hre)], axis=1))
    half = inner_product(high, low, inner_ref)
    pairs = [
        spread(half[c * NB : (c + 1) * NB, :NB], half[c * NB : (c + 1) * NB, NB:], turn_ref, 0)
        for c in range(4)
    ]
    high, low = [jnp.concatenate(part, axis=1) for part in zip(*pairs)]
    copies[5].wait()
    y = dot(back_ref[0], high) + (dot(back_ref[0], low) + dot(back_ref[1], high))
    for n in range(8):
        wide_ref[pl.ds(n, NB, stride=8), :] = y[:, n * LANES : (n + 1) * LANES]
    out_ref[...] = wide_ref[...].astype(out_ref.dtype)


def output_kernel(place_ref, mixed_ref, w_ref, out_ref, wide_ref):
    count = out_ref.shape[0] // NB
    for j in range(count):
        wide_ref[j] = mixed_ref[pl.ds(NB * j, NB), :].astype(F32)
    rows, weights = [], []
    for rel in range(2):
        for z in range(count // 2):
            j = 2 * z + (place_ref[0] + rel) % 2
            weights.append(weight_rows(place_ref, w_ref, z, count, rel * count // 2))
            for c in range(4):
                rows.append(
                    jnp.concatenate(
                        [wide_ref[j, pl.ds(c * 2 + half, 32, stride=8), :] for half in range(2)],
                        axis=1,
                    )
                )
    mixed = jnp.concatenate(rows, axis=0).astype(BF)
    result = dot(mixed, jnp.concatenate(weights, axis=0), ((0,), (0,))).astype(out_ref.dtype)
    for j in range(count):
        out_ref[pl.ds(NB * j, NB), :] = result[:, j * LANES : (j + 1) * LANES]


def call(kernel, shape, dtype, wide, flops, *args, scalars=False, fetched=None, limit=VMEM_LIMIT):
    size = sum(a.size * a.dtype.itemsize for a in args) + math.prod(shape) * 4
    space = pltpu.VMEM if fetched is None else pl.ANY
    specs = [pl.BlockSpec(memory_space=space)] * len(args)
    if scalars:
        specs[0] = pl.BlockSpec(memory_space=pltpu.SMEM)
    scratch = [pltpu.VMEM(wide, F32)]
    if fetched is not None:
        scratch = scratch + fetched
    return pl.pallas_call(
        kernel,
        out_shape=jax.ShapeDtypeStruct(shape, dtype),
        in_specs=specs,
        out_specs=pl.BlockSpec(memory_space=pltpu.VMEM),
        scratch_shapes=scratch,
        compiler_params=pltpu.CompilerParams(
            vmem_limit_bytes=limit
        ),
        cost_estimate=pl.CostEstimate(flops=flops, bytes_accessed=size, transcendentals=0),
    )(*args)


def over_z(x, step):
    return lax.ppermute(x, "ch", [(n, (n + 2 * step) % 8) for n in range(8)])


def over_core(x):
    return lax.ppermute(x, "ch", [(n, n ^ 1) for n in range(8)])


def over_plane(x, step_y, step_x):
    pairs = []
    for n in range(32):
        y, rest = divmod(n, 8)
        x_place, z_low = divmod(rest, 2)
        pairs.append((n, (y + step_y) % 4 * 8 + (x_place + step_x) % 4 * 2 + z_low))
    return lax.ppermute(x, "ctx", pairs)


def gather_z(rows):
    return jnp.concatenate([rows, over_z(rows, 1), over_z(rows, 2), over_z(rows, -1)])


def gather_plane(rows):
    return jnp.concatenate(
        [rows, over_plane(rows, 0, 1), over_plane(rows, 1, 0), over_plane(rows, 0, -1)]
    )


def local(tokens, w_in, filters, w_filter, w_out):
    ctx_count, ch_count = lax.axis_size("ctx"), lax.axis_size("ch")
    ctx_place, ch_place = lax.axis_index("ctx"), lax.axis_index("ch")
    every = ("ch", "ctx")
    outer, outer_x, inner, back, turn = tables(ctx_count, ch_count)
    wide = tokens.shape
    blocks = (ch_count, wide[0] // ch_count, wide[1])
    quarter = (ctx_place // 2 % 4 + 2 * (ctx_place // 8)) % 4
    place = jnp.stack([ch_place % 2, ch_place // 2, quarter]).astype(jnp.int32)
    in_own = gather_plane(gather_z(lax.dynamic_slice_in_dim(w_in, 32 * quarter, 32, 1).T))
    in_mate = over_core(in_own)
    tokens = lax.all_to_all(tokens, "ch", 0, 0, tiled=True)
    shaped = call(shape_kernel, wide, BF, wide, 2**25, filters, w_filter)
    shaped = lax.all_to_all(shaped, "ctx", 0, 0, tiled=True)
    spectrum = call(
        filter_kernel, (4 * NB, 2 * NB), F32, wide, 2**31, shaped, outer, inner, turn
    )
    signal = call(
        project_kernel, wide, BF, blocks, 2**29, place, tokens, in_own, in_mate, scalars=True
    )
    w_out, signal = lax.optimization_barrier((w_out, signal))
    out_rows = gather_z(lax.dynamic_slice_in_dim(w_out, 32 * quarter, 32, 0))
    out_rows = jnp.concatenate([out_rows, over_core(out_rows)])
    signal = lax.all_to_all(signal, every, 0, 0, tiled=True)
    operands = [signal, outer_x, turn, inner, spectrum, back]
    fetched = [pltpu.VMEM(a.shape, a.dtype) for a in operands] + [pltpu.SemaphoreType.DMA((6,))]
    mixed = call(
        conv_kernel, wide, BF, wide, 2**32, *operands, fetched=fetched, limit=60 * 2**20
    )
    out_rows, mixed = lax.optimization_barrier((out_rows, mixed))
    w_out = gather_plane(out_rows)
    mixed = lax.all_to_all(mixed, every, 0, 0, tiled=True)
    mixed, w_out = lax.optimization_barrier((mixed, w_out))
    result = call(
        output_kernel, wide, BF, blocks, 2**29, place, mixed, w_out, scalars=True
    )
    return lax.all_to_all(result, "ch", 0, 0, tiled=True)


def solution(mesh):
    placed = (P("ctx", "ch"), P(None, "ch"), P("ctx", None), P(None, "ch"), P("ch", None))
    return jax.shard_map(
        local, mesh=mesh, in_specs=placed, out_specs=P("ctx", "ch"), check_vma=False
    )
```
